32 devices in a mesh: groups: 1, tensor: 32 (over z, y, x, core).
Axes of the slice: x: 2, y: 2, z: 4, core: 2. Of those that a mesh axis runs over, the one named last changes fastest.
Arguments:
- incoming_hidden: bfloat16 [2, 8, 5120], P(None, 'groups'), may hold values from -6 to 6
- norm_weight_vector: float32 [5120], replicated, may hold values from 0.25 to 1.75
- query_matrix: bfloat16 [5120, 8192], P('tensor'), may hold values from -0.078125 to 0.078125
- key_matrix: bfloat16 [5120, 1024], P('tensor'), may hold values from -0.078125 to 0.078125
- value_matrix: bfloat16 [5120, 1024], P('tensor'), may hold values from -0.625 to 0.625
- output_matrix: bfloat16 [8192, 5120], P('tensor'), may hold values from -0.125 to 0.125
- query_adapter_input: bfloat16 [128, 5120], P('tensor'), may hold values from -0.078125 to 0.078125
- query_adapter_output: bfloat16 [128, 8192], P('tensor'), may hold values from -1 to 1
- output_adapter_input: bfloat16 [128, 8192], P('tensor'), may hold values from -0.0625 to 0.0625
- output_adapter_output: bfloat16 [128, 5120], P('tensor'), may hold values from -1 to 1
- objective_numerators: int32 [4], P('groups'), may hold values from 1 to 16
- lengths: int32 [8], P('groups'), may hold values from 64 to 1024, as said below
- stored_keys: bfloat16 [8, 1024, 1024], P('groups', 'tensor'), may hold values from -320 to 320, as said below
- stored_values: bfloat16 [8, 1024, 1024], P('groups', 'tensor'), may hold values from -6 to 6
Outputs:
- query_with_adapters: bfloat16 [5120, 8192], P(('groups', 'tensor'))
- output_with_adapters: bfloat16 [8192, 5120], P('tensor', 'groups')
- attended: bfloat16 [2, 8, 5120], P(None, 'groups', 'tensor')
The draws below stay inside these ranges and needn't reach their ends.
Inputs may be any that keep to these rules, and one draw needn't show every extreme that they name: The new tokens of a row stand at positions lengths and lengths + 1. `stored_keys`: the cached keys already carry their positions' rotation.
All inputs are finite; a program needn't handle non-finite values.
Results may differ from the reference program's by a relative error of at most 0.0085.
The reference program's roundings to bfloat16 on the way count: a program that leaves them out, or rounds other values in their place, can miss the bound.
Values may be sent and summed in bfloat16 or wider, within the bound.
A program may use at most 192 MiB of HBM per device.

```python
import jax
import jax.numpy as jnp
from jax import lax

MODEL_WIDTH = 5120
HEADS = 64
KVH = 8
HD = 128
ADAPTER_RANK = 32
OBJ = 4
WEIGHT_DIVISOR = 16
STEPS = 2
ROWS = 8
CTX_DEV = 32
QUERY_COLUMNS = 8192
KVDIM = 1024
ADAPTER_ROWS = 128
CTX = 1024
N_TENSOR = 32


def draw_lengths(key, part):
    key = jax.random.fold_in(key, 11)
    first_key, second_key = jax.random.split(key)
    drawn = jax.random.randint(first_key, (ROWS,), CTX // 16, CTX + 1)
    chosen = jax.random.randint(second_key, (), 0, ROWS)
    rows_index = jnp.arange(ROWS)
    drawn = jnp.where(rows_index == chosen, CTX, drawn)
    drawn = jnp.where(rows_index == (chosen + 1) % ROWS, CTX // 16, drawn)
    return drawn.astype(jnp.int32)


def draw_stored_keys(key, part):
    key = jax.random.fold_in(key, 5)
    normal_key = jax.random.fold_in(key, 0)
    base = jnp.clip(jax.random.normal(normal_key, (ROWS, CTX, KVDIM), jnp.float32), -4.0, 4.0) * 2.0
    return base.astype(jnp.bfloat16)


def plant(values, rng, least, largest):
    longest = values.shape.index(max(values.shape))
    spots = []
    for shift in (0, 1):
        where = [jax.random.randint(jax.random.fold_in(rng, axis), (), 0, length) for axis, length in enumerate(values.shape)]
        where[longest] = (where[longest] + shift) % values.shape[longest]
        spots.append(tuple(where))
    return values.at[spots[0]].set(least).at[spots[1]].set(largest)


def with_spikes(array, rng, source, target, blocks, factor):
    owner, partner = [(jnp.arange(array.shape[position]) // (array.shape[position] // blocks)).reshape([-1 if axis == position else 1 for axis in range(array.ndim)]) for position in (source, target)]
    chosen = jax.random.permutation(rng, blocks)[partner]
    strong = (owner == chosen) | (owner == (partner + blocks // 2) % blocks)
    return jnp.where(strong, factor * array, array)


def shard_levels(stream_key, extent, cuts, smallest, top_value):
    def one(position, blocks):
        heights = jax.random.uniform(jax.random.fold_in(jax.random.fold_in(stream_key, 6), position), (blocks,), jnp.float32, smallest / len(cuts), top_value / len(cuts))
        return jnp.repeat(jnp.exp(heights), extent[position] // blocks).reshape((-1,) + (1,) * (len(extent) - position - 1))

    level = one(*cuts[0])
    for cut in cuts[1:]:
        level = level * one(*cut)
    return level


def scatter_about(rng, dims, deviation, bound, cuts=(), kind=jnp.bfloat16):
    entries = jax.random.normal(rng, dims, jnp.float32) * deviation
    if len(cuts) > 0:
        entries = shard_levels(rng, dims, cuts, -0.22, 0.18) * entries
    return jnp.clip(entries, min=-bound, max=bound).astype(kind)


def gaussian_with(key, dims, spread, reach, cuts, heavy, held_as=jnp.bfloat16):
    array = spread * jax.random.normal(key, dims, jnp.float32)
    if cuts:
        array = array * shard_levels(key, dims, cuts, -0.22, 0.18)
    return jnp.clip(with_spikes(array, jax.random.fold_in(key, 3), *heavy), -reach, reach).astype(held_as)


def setup_inputs(seed: int = 0, part: int = 0) -> dict:
    splits = jax.random.split(jax.random.key(seed), 15)
    part_splits = jax.random.split(jax.random.fold_in(splits[14], part), 15)
    incoming_hidden = scatter_about(part_splits[0], (STEPS, ROWS, MODEL_WIDTH), 1.0, 6.0)
    norm_weight_vector = jnp.clip(1.0 + 0.15 * jax.random.normal(splits[1], (MODEL_WIDTH,), jnp.float32), 0.25, 1.75)
    query_matrix = scatter_about(splits[2], (MODEL_WIDTH, QUERY_COLUMNS), MODEL_WIDTH ** -0.5, 0.078125, ((0, 32),))
    key_matrix = scatter_about(splits[3], (MODEL_WIDTH, KVDIM), MODEL_WIDTH ** -0.5, 0.078125, ((0, 32),))
    value_matrix = scatter_about(splits[4], (MODEL_WIDTH, KVDIM), (MODEL_WIDTH // 64) ** -0.5, 0.625, ((0, 32),))
    output_matrix = gaussian_with(splits[5], (QUERY_COLUMNS, MODEL_WIDTH), QUERY_COLUMNS ** -0.5, 0.125, ((0, 32),), (0, 1, 32, 2.75))
    query_adapter_input = scatter_about(splits[6], (ADAPTER_ROWS, MODEL_WIDTH), MODEL_WIDTH ** -0.5, 0.078125, ((0, 32),))
    query_adapter_output = scatter_about(splits[7], (ADAPTER_ROWS, QUERY_COLUMNS), ADAPTER_RANK ** -0.5, 1.0, ((0, 32),))
    output_adapter_input = scatter_about(splits[8], (ADAPTER_ROWS, QUERY_COLUMNS), QUERY_COLUMNS ** -0.5, 0.0625, ((0, 32),))
    output_adapter_output = scatter_about(splits[9], (ADAPTER_ROWS, MODEL_WIDTH), ADAPTER_RANK ** -0.5, 1.0, ((0, 32),))
    objective_numerators = plant(jax.random.randint(part_splits[10], (OBJ,), 1, 17), jax.random.fold_in(part_splits[10], 1), 1, 16).astype(jnp.int32)
    lengths = draw_lengths(jax.random.fold_in(jax.random.fold_in(splits[14], part), 71), part)
    stored_keys = draw_stored_keys(jax.random.fold_in(jax.random.fold_in(splits[14], part), 71), part)
    stored_values = scatter_about(part_splits[13], (ROWS, CTX, KVDIM), 1.0, 6.0, ((1, 32),))
    return {"incoming_hidden": incoming_hidden, "norm_weight_vector": norm_weight_vector, "query_matrix": query_matrix, "key_matrix": key_matrix, "value_matrix": value_matrix, "output_matrix": output_matrix, "query_adapter_input": query_adapter_input, "query_adapter_output": query_adapter_output, "output_adapter_input": output_adapter_input, "output_adapter_output": output_adapter_output, "objective_numerators": objective_numerators, "lengths": lengths, "stored_keys": stored_keys, "stored_values": stored_values}


ADAPTER_SCALE = 2.0
THETA = 1000000.0
EPS = 1e-06
NEG = -1e+30
HIGHEST = lax.Precision.HIGHEST

def rotate(values, positions):
    half = values.shape[-1] // 2
    frequency = THETA ** (-2.0 * jnp.arange(half, dtype=jnp.float32) / values.shape[-1])
    angle = positions.astype(jnp.float32)[..., None, None] * frequency
    cosine = jnp.cos(angle)
    sine = jnp.sin(angle)
    leading = values[..., :half]
    trailing = values[..., half:]
    return jnp.concatenate([leading * cosine - trailing * sine, trailing * cosine + leading * sine], axis=-1)

def widen_heads(left, right, objective_mixture):
    row_scale = jnp.repeat(objective_mixture, ADAPTER_RANK)
    scaled = (left.astype(jnp.float32) * row_scale[:, None]).astype(jnp.bfloat16)
    return jnp.dot(scaled.T, right, preferred_element_type=jnp.float32)

def join_blocks(earlier, later):
    top = jnp.maximum(earlier[0], later[0])
    first_scale = jnp.exp(earlier[0] - top)
    second_scale = jnp.exp(later[0] - top)
    return (top, earlier[1] * first_scale + later[1] * second_scale, earlier[2] * first_scale[..., None] + later[2] * second_scale[..., None])

def finish(block_max, block_sum, block_out, fresh_scores, fresh_values):
    top = jnp.maximum(block_max, lax.optimization_barrier(jnp.max(fresh_scores, axis=-1)))
    carried = jnp.exp(block_max - top)
    fresh = jnp.exp(fresh_scores - top[..., None])
    denominator = block_sum * carried + lax.optimization_barrier(jnp.sum(fresh, axis=-1))
    moved = jnp.moveaxis(fresh_values.astype(jnp.float32), 0, 2)
    upper_part = block_out * carried[..., None] + lax.optimization_barrier(jnp.sum(fresh[..., None] * moved[None], axis=3))
    return (upper_part / denominator[..., None]).astype(jnp.bfloat16)

def to_groups(stats):
    return jnp.repeat(stats.reshape(stats.shape[0], stats.shape[1], HEADS), 2, axis=2)

def reference(incoming_hidden, norm_weight_vector, query_matrix, key_matrix, value_matrix, output_matrix, query_adapter_input, query_adapter_output, output_adapter_input, output_adapter_output, objective_numerators, lengths, stored_keys, stored_values):
    objective_mixture = objective_numerators.astype(jnp.float32) * (ADAPTER_SCALE / WEIGHT_DIVISOR)
    query_with_adapters = (query_matrix.astype(jnp.float32) + widen_heads(query_adapter_input, query_adapter_output, objective_mixture)).astype(jnp.bfloat16)
    output_with_adapters = (output_matrix.astype(jnp.float32) + widen_heads(output_adapter_input, output_adapter_output, objective_mixture)).astype(jnp.bfloat16)
    group = HEADS // KVH
    hidden = incoming_hidden.astype(jnp.float32)
    normed = (hidden * lax.rsqrt(lax.optimization_barrier(jnp.mean(hidden * hidden, axis=-1, keepdims=True)) + EPS) * norm_weight_vector).astype(jnp.bfloat16)
    flat = normed.reshape(STEPS * ROWS, MODEL_WIDTH)
    queries = jnp.dot(flat, query_with_adapters, preferred_element_type=jnp.float32).astype(jnp.bfloat16).reshape(STEPS, ROWS, HEADS, HD)
    new_keys = jnp.dot(flat, key_matrix, preferred_element_type=jnp.float32).astype(jnp.bfloat16).reshape(STEPS, ROWS, KVH, HD)
    new_values = jnp.dot(flat, value_matrix, preferred_element_type=jnp.float32).astype(jnp.bfloat16).reshape(STEPS, ROWS, KVH, HD)
    positions = lengths[None, :] + jnp.arange(STEPS, dtype=jnp.int32)[:, None]
    rotated_queries = rotate(queries.astype(jnp.float32), positions).astype(jnp.bfloat16).reshape(STEPS, ROWS, KVH, group, HD)
    rotated_keys = rotate(new_keys.astype(jnp.float32), positions).astype(jnp.bfloat16)
    query_float = rotated_queries.astype(jnp.float32)
    key_blocks = stored_keys.reshape(ROWS, N_TENSOR, CTX_DEV, KVH, HD)
    value_blocks = stored_values.reshape(ROWS, N_TENSOR, CTX_DEV, KVH, HD)
    scale = HD ** (-0.5)

    def visit(carry, block):
        keys = lax.dynamic_index_in_dim(key_blocks, block, 1, keepdims=False).astype(jnp.float32)
        values = lax.dynamic_index_in_dim(value_blocks, block, 1, keepdims=False).astype(jnp.float32)
        offsets = block * CTX_DEV + jnp.arange(CTX_DEV, dtype=jnp.int32)
        valid = offsets[None, :] < lengths[:, None]
        scores = jnp.einsum('srkgh,rpkh->srkgp', query_float, keys, precision=HIGHEST) * scale
        masked = jnp.where(valid[None, :, None, None, :], scores, NEG)
        block_max = lax.optimization_barrier(jnp.max(masked, axis=-1))
        block_exp = jnp.exp(masked - block_max[..., None]) * valid.astype(jnp.float32)[None, :, None, None, :]
        block_sum = lax.optimization_barrier(jnp.sum(block_exp, axis=-1))
        block_weights = lax.optimization_barrier(block_exp.astype(jnp.bfloat16)).astype(jnp.float32)
        block_out = jnp.einsum('srkgp,rpkh->srkgh', block_weights, values, precision=HIGHEST)
        return (join_blocks(carry, (block_max, block_sum, block_out)), None)
    shape = (STEPS, ROWS, KVH, group)
    start = (jnp.full(shape, NEG, jnp.float32), jnp.zeros(shape, jnp.float32), jnp.zeros(shape + (HD,), jnp.float32))
    (block_max, block_sum, block_out), unused = lax.scan(visit, start, jnp.arange(N_TENSOR, dtype=jnp.int32))
    fresh_scores = jnp.einsum('srkgh,trkh->srkgt', query_float, rotated_keys.astype(jnp.float32), precision=HIGHEST) * scale
    later = jnp.arange(STEPS, dtype=jnp.int32)[None, :] > jnp.arange(STEPS, dtype=jnp.int32)[:, None]
    fresh_scores = jnp.where(later[:, None, None, None, :], NEG, fresh_scores)
    fresh_groups = jnp.repeat(fresh_scores.reshape(STEPS, ROWS, HEADS, STEPS), 2, axis=2)
    value_groups = jnp.repeat(new_values, group, axis=2).reshape(STEPS, ROWS, 2 * HEADS, HD // 2)
    attention = finish(to_groups(block_max), to_groups(block_sum), block_out.reshape(STEPS, ROWS, 2 * HEADS, HD // 2), fresh_groups, value_groups)
    attended = jnp.dot(attention.reshape(STEPS * ROWS, QUERY_COLUMNS), output_with_adapters, preferred_element_type=jnp.float32)
    return (query_with_adapters, output_with_adapters, attended.astype(jnp.bfloat16).reshape(STEPS, ROWS, MODEL_WIDTH))
```

```python
import jax
import jax.numpy as jnp
from jax import lax
from jax.sharding import PartitionSpec as P

HEADS = 64
KVH = 8
HD = 128
ADAPTER_RANK = 32
WEIGHT_DIVISOR = 16


ADAPTER_SCALE = 2.0
THETA = 1000000.0
EPS = 1e-06
NEG = -1e30


def rotate(values, positions):
    half = values.shape[-1] // 2
    frequency = THETA ** (-2.0 * jnp.arange(half, dtype=jnp.float32) / values.shape[-1])
    angle = positions.astype(jnp.float32)[..., None, None] * frequency
    cosine = jnp.cos(angle)
    sine = jnp.sin(angle)
    leading = values[..., :half]
    trailing = values[..., half:]
    return jnp.concatenate(
        [leading * cosine - trailing * sine, trailing * cosine + leading * sine], axis=-1
    )


def widen_heads(left, right, row_scale):
    scaled = (left.astype(jnp.float32) * row_scale[:, None]).astype(jnp.bfloat16)
    return lax.dot_general(
        scaled, right, (((0,), (0,)), ((), ())), preferred_element_type=jnp.float32
    )


def finish(block_max, block_sum, block_out, fresh_scores, fresh_values):
    top = jnp.maximum(block_max, jnp.max(fresh_scores, axis=-1))
    carried = jnp.exp(block_max - top)
    fresh = jnp.exp(fresh_scores - top[..., None])
    denominator = block_sum * carried + jnp.sum(fresh, axis=-1)
    moved = jnp.moveaxis(fresh_values.astype(jnp.float32), 0, 2)
    upper_part = block_out * carried[..., None] + jnp.sum(fresh[..., None] * moved[None], axis=3)
    return (upper_part / denominator[..., None]).astype(jnp.bfloat16)


def local(
    incoming_hidden,
    norm_weight_vector,
    query_matrix,
    key_matrix,
    value_matrix,
    output_matrix,
    query_adapter_input,
    query_adapter_output,
    output_adapter_input,
    output_adapter_output,
    objective_numerators,
    lengths,
    stored_keys,
    stored_values,
):
    count = lax.axis_size("tensor")
    shard = lax.axis_index("tensor")
    group = HEADS // KVH
    width = 2 * HEADS // count
    scale = HD ** (-0.5)
    objective_mixture = objective_numerators.astype(jnp.float32) * (ADAPTER_SCALE / WEIGHT_DIVISOR)
    row_scale = jnp.repeat(objective_mixture, ADAPTER_RANK)
    query_in_cols, output_in_cols = (
        lax.all_to_all(query_adapter_input, "tensor", split_axis=1, concat_axis=0, tiled=True),
        lax.all_to_all(output_adapter_input, "tensor", split_axis=1, concat_axis=0, tiled=True),
    )
    query_out_all, output_out_all = (
        lax.all_gather(query_adapter_output, "tensor", axis=0, tiled=True),
        lax.all_gather(output_adapter_output, "tensor", axis=0, tiled=True),
    )
    query_with_adapters = (
        query_matrix.astype(jnp.float32) + widen_heads(query_in_cols, query_out_all, row_scale)
    ).astype(jnp.bfloat16)
    output_with_adapters = (
        output_matrix.astype(jnp.float32) + widen_heads(output_in_cols, output_out_all, row_scale)
    ).astype(jnp.bfloat16)
    rows = incoming_hidden.shape[1]
    features_here = query_matrix.shape[0]
    cache_len = stored_keys.shape[1]
    keys_cache = stored_keys.reshape(rows, cache_len, KVH, HD)
    values_cache = stored_values.reshape(rows, cache_len, KVH, HD)
    offsets = shard * cache_len + jnp.arange(cache_len, dtype=jnp.int32)
    valid = offsets[None, :] < lengths[:, None]
    valid_float = valid.astype(jnp.float32)[None, :, None, None, :]
    results = []
    earlier_keys = []
    earlier_values = []
    for position in range(1):
        block = incoming_hidden
        project_steps_here = block.shape[0]
        values_in = block.astype(jnp.float32)
        normed = (
            values_in
            * lax.rsqrt(jnp.mean(values_in * values_in, axis=-1, keepdims=True) + EPS)
            * norm_weight_vector
        ).astype(jnp.bfloat16)
        own_features = lax.dynamic_slice_in_dim(normed, shard * features_here, features_here, 2)
        query_part = jnp.einsum(
            "srd,dc->src", own_features, query_with_adapters, preferred_element_type=jnp.float32
        )
        key_part = jnp.einsum(
            "srd,dc->src", own_features, key_matrix, preferred_element_type=jnp.float32
        )
        value_part = jnp.einsum(
            "srd,dc->src", own_features, value_matrix, preferred_element_type=jnp.float32
        )
        queries, new_keys, new_values = lax.psum((query_part, key_part, value_part), "tensor")
        queries = queries.astype(jnp.bfloat16)
        new_keys = new_keys.astype(jnp.bfloat16)
        new_values = new_values.astype(jnp.bfloat16)
        positions = (
            lengths[None, :] + position + jnp.arange(project_steps_here, dtype=jnp.int32)[:, None]
        )
        project_rotated_queries = rotate(
            queries.reshape(project_steps_here, rows, HEADS, HD).astype(jnp.float32), positions
        ).astype(jnp.bfloat16)
        rotated_keys = rotate(
            new_keys.reshape(project_steps_here, rows, KVH, HD).astype(jnp.float32), positions
        ).astype(jnp.bfloat16)
        rotated_queries, rotated_keys, new_values = (
            project_rotated_queries,
            rotated_keys,
            new_values.reshape(project_steps_here, rows, KVH, HD),
        )
        earlier_keys.append(rotated_keys)
        earlier_values.append(new_values)
        fresh_keys = jnp.concatenate(earlier_keys, axis=0)
        steps_here = rotated_queries.shape[0]
        tokens_new = fresh_keys.shape[0]
        grouped = rotated_queries.reshape(steps_here, rows, KVH, group, HD)
        scores = (
            jnp.einsum("srkgh,rpkh->srkgp", grouped, keys_cache, preferred_element_type=jnp.float32)
            * scale
        )
        masked = jnp.where(valid[None, :, None, None, :], scores, NEG)
        block_max = jnp.max(masked, axis=-1)
        block_exp = jnp.exp(masked - block_max[..., None]) * valid_float
        block_sum = jnp.sum(block_exp, axis=-1)
        block_out = jnp.einsum(
            "srkgp,rpkh->srkgh",
            block_exp.astype(jnp.bfloat16),
            values_cache,
            preferred_element_type=jnp.float32,
        )
        group_max = jnp.repeat(block_max.reshape(steps_here, rows, HEADS), 2, axis=2)
        group_sum = jnp.repeat(block_sum.reshape(steps_here, rows, HEADS), 2, axis=2)
        halves = block_out.reshape(steps_here, rows, 2 * HEADS, HD // 2)
        fresh_scores = (
            jnp.einsum("srkgh,trkh->srkgt", grouped, fresh_keys, preferred_element_type=jnp.float32)
            * scale
        )
        later = (
            jnp.arange(tokens_new, dtype=jnp.int32)[None, :]
            > position + jnp.arange(steps_here, dtype=jnp.int32)[:, None]
        )
        fresh_scores = jnp.where(later[:, None, None, None, :], NEG, fresh_scores)
        fresh_groups = jnp.repeat(
            fresh_scores.reshape(steps_here, rows, HEADS, tokens_new), 2, axis=2
        )
        value_groups = jnp.repeat(jnp.concatenate(earlier_values, axis=0), group, axis=2).reshape(
            tokens_new, rows, 2 * HEADS, HD // 2
        )
        packed = jnp.concatenate([halves, group_max[..., None], group_sum[..., None]], axis=-1)
        packed = packed.reshape(steps_here, rows, count, width, HD // 2 + 2)
        packed = lax.all_to_all(packed, "tensor", split_axis=2, concat_axis=2, tiled=True)
        all_max = packed[..., HD // 2]
        top = jnp.max(all_max, axis=2)
        carry = jnp.exp(all_max - top[:, :, None])
        all_sum = jnp.sum(packed[..., HD // 2 + 1] * carry, axis=2)
        all_out = jnp.sum(packed[..., : HD // 2] * carry[..., None], axis=2)
        own_scores = lax.dynamic_slice_in_dim(fresh_groups, shard * width, width, 2)
        own_values = lax.dynamic_slice_in_dim(value_groups, shard * width, width, 2)
        finished = finish(top, all_sum, all_out, own_scores, own_values)
        attention = finished.reshape(steps_here, rows, width * (HD // 2))
        projected = jnp.einsum(
            "src,cd->srd", attention, output_with_adapters, preferred_element_type=jnp.float32
        )
        results.append(
            lax.psum_scatter(projected, "tensor", scatter_dimension=2, tiled=True).astype(
                jnp.bfloat16
            )
        )
    attended = jnp.concatenate(results, axis=0)
    return (query_with_adapters, output_with_adapters, attended)


def solution(mesh):
    placed = (
        P(None, "groups", None),
        P(),
        P("tensor", None),
        P("tensor", None),
        P("tensor", None),
        P("tensor", None),
        P("tensor", None),
        P("tensor", None),
        P("tensor", None),
        P("tensor", None),
        P("groups"),
        P("groups"),
        P("groups", "tensor", None),
        P("groups", "tensor", None),
    )
    return jax.shard_map(
        local,
        mesh=mesh,
        in_specs=placed,
        out_specs=(
            P(("groups", "tensor"), None),
            P("tensor", "groups"),
            P(None, "groups", "tensor"),
        ),
        check_vma=False,
    )
```

```python
import functools

import jax
import jax.numpy as jnp
from jax import lax
from jax.experimental import pallas as pl
from jax.experimental.pallas import tpu as pltpu
from jax.sharding import PartitionSpec as P

HEADS = 64
KVH = 8
HD = 128
ADAPTER_RANK = 32
WEIGHT_DIVISOR = 16
GROUP = HEADS // KVH
PLANE = 4

ADAPTER_SCALE = 2.0
THETA = 1000000.0
EPS = 1e-06
NEG = -1e30
F32 = jnp.float32
BF16 = jnp.bfloat16


def ceil_to(value, step):
    return -(-value // step) * step


def dot(a, b):
    return jnp.dot(a, b, preferred_element_type=F32)


def remote(src, dst, send, recv, device):
    return pltpu.make_async_remote_copy(
        src_ref=src, dst_ref=dst, send_sem=send, recv_sem=recv, device_id={"tensor": device}
    )


def each(first, last, body):
    def step(k, carry):
        body(k)
        return carry

    lax.fori_loop(first, last, step, 0)


class Gather:
    def __init__(self, buf, zsend, psend, csend, recv, place):
        self.buf, self.zsend, self.psend, self.csend, self.recv = buf, zsend, psend, csend, recv
        self.chip, self.core, self.nz = place
        self.z, self.p = self.chip // PLANE, self.chip % PLANE

    def copy(self, chip, send, device):
        block = self.buf.at[self.core, chip]
        return remote(block, block, send, self.recv.at[self.core, chip], device)

    def zcopy(self, k):
        z = (self.z + k) % self.nz
        return self.copy(self.chip, self.zsend.at[k - 1], (z * PLANE + self.p) * 2 + self.core)

    def pcopy(self, zk, k):
        chip = ((self.z + zk) % self.nz) * PLANE + self.p
        to = self.z * PLANE + (self.p + k) % PLANE
        return self.copy(chip, self.psend.at[zk, k - 1], to * 2 + self.core)

    def ccopy(self, zk, k):
        chip = ((self.z + zk) % self.nz) * PLANE + (self.p + k) % PLANE
        return self.copy(chip, self.csend.at[zk, k], self.chip * 2 + 1 - self.core)

    def first(self):
        each(1, self.nz, lambda k: self.zcopy(k).start())
        self.spread(0)

    def spread(self, zk):
        for k in range(1, PLANE):
            self.pcopy(zk, k).start()
        self.ccopy(zk, 0).start()

    def await_block(self, core, zk, k):
        chip = ((self.z + zk) % self.nz) * PLANE + (self.p + k) % PLANE
        block = self.buf.at[core, chip]
        remote(
            block, block, self.csend.at[zk, k], self.recv.at[core, chip], self.chip * 2 + 1 - self.core
        ).wait_recv()

    def second(self):
        def body(zk):
            self.await_block(self.core, zk, 0)
            self.spread(zk)

        each(1, self.nz, body)

    def third(self):
        def body(zk):
            for k in range(1, PLANE):
                self.await_block(self.core, zk, k)
                self.ccopy(zk, k).start()

        each(0, self.nz, body)

    def last(self):
        def body(zk):
            for k in range(PLANE):
                self.await_block(1 - self.core, zk, k)
                self.ccopy(zk, k).wait_send()
            for k in range(1, PLANE):
                self.pcopy(zk, k).wait_send()

        each(0, self.nz, body)
        each(1, self.nz, lambda k: self.zcopy(k).wait_send())


class Exchange:
    def __init__(self, part, other, joined, landed, one, send, recv, place):
        self.part, self.other, self.joined, self.landed = part, other, joined, landed
        self.one, self.send, self.recv = one, send, recv
        self.chip, self.core, unused = place
        self.count = landed.shape[0]

    def inside(self):
        return remote(
            self.part.at[1 - self.core],
            self.other,
            self.one.at[0],
            self.one.at[1],
            self.chip * 2 + 1 - self.core,
        )

    def outside(self, k):
        to = (self.chip + k) % self.count
        return remote(
            self.joined.at[to],
            self.landed.at[self.chip],
            self.send.at[k],
            self.recv.at[self.chip],
            to * 2 + self.core,
        )

    def arrival(self, k):
        origin = (self.chip + self.count - k) % self.count
        return remote(
            self.joined.at[origin],
            self.landed.at[origin],
            self.send.at[k],
            self.recv.at[origin],
            origin * 2 + self.core,
        )

    def go(self, join):
        self.inside().wait_recv()
        self.joined[...] = join(self.part[self.core], self.other[...])
        each(1, self.count, lambda k: self.outside(k).start())
        self.landed[self.chip] = self.joined[self.chip]

    def finish(self):
        each(1, self.count, lambda k: self.arrival(k).wait_recv())

    def drain(self):
        self.inside().wait_send()
        each(1, self.count, lambda k: self.outside(k).wait_send())


def join_blocks(a, b, width):
    outs = []
    lane = lax.broadcasted_iota(jnp.int32, a.shape[:2] + (128,), 2)
    stats = jnp.zeros(a.shape[:2] + (128,), F32)
    for j in range(width // HD):
        ma, mb = a[:, :, width + j : width + j + 1], b[:, :, width + j : width + j + 1]
        sa, sb = (
            a[:, :, width + 64 + j : width + 65 + j],
            b[:, :, width + 64 + j : width + 65 + j],
        )
        top = jnp.maximum(ma, mb)
        ca, cb = jnp.exp(ma - top), jnp.exp(mb - top)
        outs.append(a[:, :, j * HD : (j + 1) * HD] * ca + b[:, :, j * HD : (j + 1) * HD] * cb)
        stats = jnp.where(lane == j, top, stats)
        stats = jnp.where(lane == 64 + j, sa * ca + sb * cb, stats)
    return jnp.concatenate(outs + [stats], axis=-1)


def rotated(values, cosine, sine):
    return values * cosine + jnp.concatenate([values[:, 64:], values[:, :64]], axis=1) * sine


def kernel(
    count,
    qw,
    x_ref,
    wq_ref,
    wk_ref,
    wv_ref,
    wo_ref,
    a_ref,
    bq_ref,
    bo_ref,
    cos_ref,
    sin_ref,
    valid_ref,
    k_ref,
    v_ref,
    qout_ref,
    oout_ref,
    att_ref,
    ra,
    rq,
    ro,
    qg,
    q_part,
    q_other,
    q_joined,
    q_landed,
    kv_part,
    kv_other,
    kv_joined,
    kv_landed,
    m_part,
    m_other,
    m_joined,
    m_landed,
    o_part,
    o_other,
    o_joined,
    o_landed,
    a_send,
    a_recv,
    rq_z,
    rq_p,
    rq_c,
    rq_recv,
    ro_z,
    ro_p,
    ro_c,
    ro_recv,
    g_send,
    g_recv,
    ex_one,
    ex_send,
    ex_recv,
):
    me = lax.axis_index("tensor")
    chip, core = me // 2, me % 2
    chips = count // 2
    place = (chip, core, chips // PLANE)
    sibling = chip * 2 + 1 - core
    fq, fo = wq_ref.shape[0], wo_ref.shape[0]
    columns, width = wq_ref.shape[1], wo_ref.shape[1]
    chunks = 16 // (128 // count)
    rows = count * 16

    barrier = pltpu.get_barrier_semaphore()
    each(
        1,
        count,
        lambda k: pl.semaphore_signal(
            barrier, inc=1, device_id={"tensor": (me + k) % count}
        ),
    )
    pl.semaphore_wait(barrier, count - 1)

    gq = Gather(rq, rq_z, rq_p, rq_c, rq_recv, place)
    go = Gather(ro, ro_z, ro_p, ro_c, ro_recv, place)
    rq[core, chip] = bq_ref[...]
    ro[core, chip] = bo_ref[...]
    ra[core, chip] = a_ref[me]
    gq.first()

    def acopy(k):
        to = (me + k) % count
        return remote(a_ref.at[to], ra.at[core, chip], a_send.at[k], a_recv.at[me], to)

    def aarrival(k):
        origin = (me + count - k) % count
        return remote(
            a_ref.at[origin],
            ra.at[origin % 2, origin // 2],
            a_send.at[k],
            a_recv.at[origin],
            origin,
        )

    each(1, count, lambda k: acopy(k).start())
    gq.second()
    go.first()
    gq.third()
    go.second()
    each(1, count, lambda k: aarrival(k).wait_recv())
    factors = ra[...].reshape(rows, 128).astype(F32).T
    lane = lax.broadcasted_iota(jnp.int32, (128, rows), 1)

    def left(block, chunk, height):
        moved = factors if chunk == block else pltpu.roll(factors, (chunk - block) % rows, 1)
        return jnp.where(lane % chunks == chunk, moved, 0.0).astype(BF16)[:height]

    def merge(base, out, gathered, features, skip):
        step = gathered.shape[3]
        for block in range(ceil_to(features, 128) // 128):
            low = block * 128
            high = min(features, low + 128)
            for chunk in range(chunks):
                lhs = left(skip + block, chunk, high - low)
                part = step // max(1, step // 512)
                for at in range(0, step, part):
                    right = gathered[:, :, :, at : at + part].reshape(rows, part)
                    span = slice(chunk * step + at, chunk * step + at + part)
                    out[low:high, span] = (base[low:high, span].astype(F32) + dot(lhs, right)).astype(
                        BF16
                    )

    gq.last()
    merge(wq_ref, qout_ref, rq, fq, 0)

    ex_q = Exchange(q_part, q_other, q_joined, q_landed, ex_one.at[0], ex_send.at[0], ex_recv.at[0], place)
    ex_kv = Exchange(
        kv_part, kv_other, kv_joined, kv_landed, ex_one.at[1], ex_send.at[1], ex_recv.at[1], place
    )
    ex_m = Exchange(m_part, m_other, m_joined, m_landed, ex_one.at[2], ex_send.at[2], ex_recv.at[2], place)
    ex_o = Exchange(o_part, o_other, o_joined, o_landed, ex_one.at[3], ex_send.at[3], ex_recv.at[3], place)

    x = x_ref[...]
    for d in range(count):
        head = d * HEADS // count
        q_part[d % 2, d // 2] = dot(x, qout_ref[:, head * HD : head * HD + qw])
    ex_q.inside().start()
    new_k = dot(x, wk_ref[...])
    new_v = dot(x, wv_ref[...])
    for d in range(count):
        g = d * HEADS // count // GROUP
        kv_part[d % 2, d // 2] = jnp.concatenate(
            [new_k[:, g * HD : (g + 1) * HD], new_v[:, g * HD : (g + 1) * HD]], axis=1
        )
    ex_q.go(lambda a, b: a + b)
    ex_kv.inside().start()
    go.third()
    ex_kv.go(lambda a, b: a + b)
    o_part[...] = jnp.zeros(o_part.shape, F32)
    ex_q.finish()
    cosine, sine = cos_ref[...], sin_ref[...]
    query = jnp.sum(q_landed[...], axis=0).astype(BF16).astype(F32)
    query = jnp.concatenate(
        [rotated(query[:, j * HD : (j + 1) * HD], cosine, sine) for j in range(qw // HD)], axis=1
    ).astype(BF16)
    qg[core, chip] = query

    def gcopy(k):
        to = (chip + k) % chips
        block = qg.at[core, chip]
        return remote(block, block, g_send.at[k], g_recv.at[chip], to * 2 + core)

    def garrival(k):
        origin = (chip + chips - k) % chips
        block = qg.at[core, origin]
        return remote(block, block, g_send.at[k], g_recv.at[origin], origin * 2 + core)

    gin = remote(qg.at[core], qg.at[core], g_send.at[0], g_recv.at[chips], sibling)
    gout = remote(qg.at[1 - core], qg.at[1 - core], g_send.at[0], g_recv.at[chips], sibling)
    each(1, chips, lambda k: gcopy(k).start())
    each(1, chips, lambda k: garrival(k).wait_recv())
    gin.start()
    gout.wait_recv()

    valid = valid_ref[...]
    scale = HD ** (-0.5)
    cached = k_ref.shape[0] * k_ref.shape[1]
    small = lax.broadcasted_iota(jnp.int32, (16, 128), 1)
    per = qw // HD
    for g in range(KVH):
        heads = []
        for h in range(g * GROUP, (g + 1) * GROUP):
            d = h * count // HEADS
            j = h - d * HEADS // count
            heads.append(qg[d % 2, d // 2, :, j * HD : (j + 1) * HD])
        keys = k_ref[:, :, g * HD : (g + 1) * HD].reshape(cached, HD)
        values = v_ref[:, :, g * HD : (g + 1) * HD].reshape(cached, HD)
        scores = (
            lax.dot_general(
                jnp.concatenate(heads, axis=0),
                keys,
                (((1,), (1,)), ((), ())),
                preferred_element_type=F32,
            )
            * scale
        )
        scores = jnp.where(valid > 0.0, scores, NEG)
        block_max = jnp.max(scores, axis=1, keepdims=True)
        block_exp = jnp.exp(scores - block_max) * valid
        block_sum = jnp.sum(block_exp, axis=1, keepdims=True)
        block_out = dot(block_exp.astype(BF16), values)
        for d in range(count):
            head = d * HEADS // count
            if head // GROUP != g:
                continue
            stats = jnp.zeros((16, 128), F32)
            pieces = []
            for j in range(per):
                span = slice((head + j - g * GROUP) * 16, (head + j - g * GROUP + 1) * 16)
                pieces.append(block_out[span])
                stats = jnp.where(small == j, block_max[span], stats)
                stats = jnp.where(small == 64 + j, block_sum[span], stats)
            m_part[d % 2, d // 2] = jnp.concatenate(pieces + [stats], axis=1)
    ex_m.inside().start()
    ex_m.go(functools.partial(join_blocks, width=qw))

    go.last()
    merge(wo_ref, oout_ref, ro, fo, ceil_to(fq, 128) // 128)

    ex_kv.finish()
    fresh = jnp.sum(kv_landed[...], axis=0).astype(BF16).astype(F32)
    new_key = rotated(fresh[:, :HD], cosine, sine).astype(BF16).astype(F32)
    new_value = fresh[:, HD:]
    row = lax.broadcasted_iota(jnp.int32, (16, 1), 0)
    twice = lambda part: jnp.concatenate([part, part], axis=0)
    k0, k1 = twice(new_key[:8]), twice(new_key[8:])
    v0, v1 = twice(new_value[:8]), twice(new_value[8:])
    ex_m.finish()
    landed = m_landed[...]
    pieces = []
    for j in range(per):
        own = query[:, j * HD : (j + 1) * HD].astype(F32)
        s0 = jnp.sum(own * k0, axis=1, keepdims=True) * scale
        s1 = jnp.sum(own * k1, axis=1, keepdims=True) * scale
        s1 = jnp.where(row < 8, NEG, s1)
        maxima = landed[:, :, qw + j : qw + j + 1]
        top = jnp.maximum(jnp.max(maxima, axis=0), jnp.maximum(s0, s1))
        carried = jnp.exp(maxima - top[None])
        e0, e1 = jnp.exp(s0 - top), jnp.exp(s1 - top)
        total = jnp.sum(landed[:, :, qw + 64 + j : qw + 65 + j] * carried, axis=0) + e0 + e1
        upper = jnp.sum(landed[:, :, j * HD : (j + 1) * HD] * carried, axis=0) + e0 * v0 + e1 * v1
        pieces.append((upper / total).astype(BF16))
    attention = jnp.concatenate(pieces, axis=1)
    if fo < qw:
        attention = jnp.where(me % (qw // fo) == 0, attention[:, :fo], attention[:, fo : 2 * fo])

    share = width // count
    for d in range(0, count, 4):
        wide = dot(attention, oout_ref[:, d * share : (d + 4) * share])
        for i in range(4):
            o_part[(d + i) % 2, (d + i) // 2, :, :share] = wide[:, i * share : (i + 1) * share]
    ex_o.inside().start()
    ex_o.go(lambda a, b: a + b)
    ex_o.finish()
    att_ref[...] = jnp.sum(o_landed[...], axis=0)[:, :share].astype(BF16)

    each(1, count, lambda k: acopy(k).wait_send())
    each(1, chips, lambda k: gcopy(k).wait_send())
    gin.wait_send()
    for exchange in (ex_q, ex_kv, ex_m, ex_o):
        exchange.drain()


def local(
    incoming_hidden,
    norm_weight_vector,
    query_matrix,
    key_matrix,
    value_matrix,
    output_matrix,
    query_adapter_input,
    query_adapter_output,
    output_adapter_input,
    output_adapter_output,
    objective_numerators,
    lengths,
    stored_keys,
    stored_values,
):
    count = lax.axis_size("tensor")
    shard = lax.axis_index("tensor")
    steps, rows, features = incoming_hidden.shape
    lines = steps * rows
    own = query_adapter_input.shape[0]
    chunks = 16 // own
    fq, fo = query_matrix.shape[0], output_matrix.shape[0]
    columns = query_matrix.shape[1]
    qw = max(HD, columns // count)
    chips = count // 2
    nz = chips // PLANE

    mixing = objective_numerators.astype(F32) * (ADAPTER_SCALE / WEIGHT_DIVISOR)
    row_scale = lax.dynamic_slice_in_dim(jnp.repeat(mixing, ADAPTER_RANK), shard * own, own)

    def blocks(factor, size):
        scaled = (factor.astype(F32) * row_scale[:, None]).astype(BF16).reshape(own, count, size)
        padded = jnp.pad(scaled, ((0, 0), (0, 0), (0, ceil_to(size, 128) - size)))
        return padded.reshape(own, count, -1, 128)

    ab = jnp.concatenate([blocks(query_adapter_input, fq), blocks(output_adapter_input, fo)], axis=2)
    ab = jnp.pad(ab, ((0, 0), (0, 0), (0, chunks - ab.shape[2]), (0, 0)))
    ab = ab.transpose(1, 0, 2, 3).reshape(count, 16, 128)
    bq = query_adapter_output.reshape(16, -1)
    bo = output_adapter_output.reshape(16, -1)

    values_in = incoming_hidden.astype(F32)
    normed = (
        values_in
        * lax.rsqrt(jnp.mean(values_in * values_in, axis=-1, keepdims=True) + EPS)
        * norm_weight_vector
    ).astype(BF16)
    x = lax.dynamic_slice_in_dim(normed.reshape(lines, features), shard * fq, fq, 1)

    half = HD // 2
    frequency = THETA ** (-2.0 * jnp.arange(half, dtype=F32) / HD)
    positions = (lengths[None, :] + jnp.arange(steps, dtype=jnp.int32)[:, None]).reshape(lines)
    angle = positions.astype(F32)[:, None] * frequency
    cosine, sine = jnp.cos(angle), jnp.sin(angle)
    cosine = jnp.concatenate([cosine, cosine], axis=1)
    sine = jnp.concatenate([-sine, sine], axis=1)

    cache = stored_keys.shape[1]
    line = jnp.arange(GROUP * lines, dtype=jnp.int32) % rows
    spot = jnp.arange(rows * cache, dtype=jnp.int32)
    inside = (shard * cache + spot % cache)[None, :] < lengths[line][:, None]
    valid = (inside & (line[:, None] == (spot // cache)[None, :])).astype(F32)

    share = output_matrix.shape[1] // count
    ow = ceil_to(share, 128)
    vmem = pl.BlockSpec(memory_space=pltpu.VMEM)
    dma = pltpu.SemaphoreType.DMA

    def exchange(width):
        return [
            pltpu.VMEM((2, chips, lines, width), F32),
            pltpu.VMEM((chips, lines, width), F32),
            pltpu.VMEM((chips, lines, width), F32),
            pltpu.VMEM((chips, lines, width), F32),
        ]

    def gather():
        return [dma((nz,)), dma((nz, PLANE)), dma((nz, PLANE)), dma((2, chips))]

    query_out, output_out, attended = pl.pallas_call(
        functools.partial(kernel, count, qw),
        out_shape=(
            jax.ShapeDtypeStruct(query_matrix.shape, BF16),
            jax.ShapeDtypeStruct(output_matrix.shape, BF16),
            jax.ShapeDtypeStruct((lines, share), BF16),
        ),
        in_specs=[vmem] * 13,
        out_specs=(vmem, vmem, vmem),
        scratch_shapes=[
            pltpu.VMEM((2, chips, 16, 128), BF16),
            pltpu.VMEM((2, chips) + bq.shape, BF16),
            pltpu.VMEM((2, chips) + bo.shape, BF16),
            pltpu.VMEM((2, chips, lines, qw), BF16),
        ]
        + exchange(qw)
        + exchange(2 * HD)
        + exchange(qw + 128)
        + exchange(ow)
        + [dma((count,)), dma((count,))]
        + gather()
        + gather()
        + [dma((chips,)), dma((chips + 1,))]
        + [dma((4, 2)), dma((4, chips)), dma((4, chips))],
        compiler_params=pltpu.CompilerParams(
            collective_id=0, has_side_effects=True, vmem_limit_bytes=56 * 1024 * 1024
        ),
    )(
        x,
        query_matrix,
        key_matrix,
        value_matrix,
        output_matrix,
        ab,
        bq,
        bo,
        cosine,
        sine,
        valid,
        stored_keys,
        stored_values,
    )
    return (query_out, output_out, attended.reshape(steps, rows, share))


def solution(mesh):
    placed = (
        P(None, "groups", None),
        P(),
        P("tensor", None),
        P("tensor", None),
        P("tensor", None),
        P("tensor", None),
        P("tensor", None),
        P("tensor", None),
        P("tensor", None),
        P("tensor", None),
        P("groups"),
        P("groups"),
        P("groups", "tensor", None),
        P("groups", "tensor", None),
    )
    return jax.shard_map(
        local,
        mesh=mesh,
        in_specs=placed,
        out_specs=(
            P(("groups", "tensor"), None),
            P("tensor", "groups"),
            P(None, "groups", "tensor"),
        ),
        check_vma=False,
    )
```

```python
import functools

import jax
import jax.numpy as jnp
import numpy as np
from jax import lax
from jax.experimental import pallas as pl
from jax.experimental.pallas import tpu as pltpu
from jax.sharding import PartitionSpec as P

HEADS = 64
KVH = 8
HD = 128
ADAPTER_RANK = 32
WEIGHT_DIVISOR = 16
GROUP = HEADS // KVH
PLANE = 4

ADAPTER_SCALE = 2.0
THETA = 1000000.0
EPS = 1e-06
NEG = -1e30
F32 = jnp.float32
BF16 = jnp.bfloat16


def ceil_to(value, step):
    return -(-value // step) * step


def dot(a, b):
    return jnp.dot(a, b, preferred_element_type=F32)


def remote(src, dst, send, recv, device):
    return pltpu.make_async_remote_copy(
        src_ref=src, dst_ref=dst, send_sem=send, recv_sem=recv, device_id={"tensor": device}
    )


def each(first, last, body):
    def step(k, carry):
        body(k)
        return carry

    lax.fori_loop(first, last, step, 0)


class Gather:
    def __init__(self, buf, zsend, psend, csend, recv, place):
        self.buf, self.zsend, self.psend, self.csend, self.recv = buf, zsend, psend, csend, recv
        self.chip, self.core, self.nz = place
        self.z, self.p = self.chip // PLANE, self.chip % PLANE

    def copy(self, chip, send, device):
        block = self.buf.at[self.core, chip]
        return remote(block, block, send, self.recv.at[self.core, chip], device)

    def zcopy(self, k):
        z = (self.z + k) % self.nz
        return self.copy(self.chip, self.zsend.at[k - 1], (z * PLANE + self.p) * 2 + self.core)

    def pcopy(self, zk, k):
        chip = ((self.z + zk) % self.nz) * PLANE + self.p
        to = self.z * PLANE + (self.p + k) % PLANE
        return self.copy(chip, self.psend.at[zk, k - 1], to * 2 + self.core)

    def ccopy(self, zk, k):
        chip = ((self.z + zk) % self.nz) * PLANE + (self.p + k) % PLANE
        return self.copy(chip, self.csend.at[zk, k], self.chip * 2 + 1 - self.core)

    def first(self):
        each(1, self.nz, lambda k: self.zcopy(k).start())
        self.spread(0)

    def spread(self, zk):
        for k in range(1, PLANE):
            self.pcopy(zk, k).start()
        self.ccopy(zk, 0).start()

    def await_block(self, core, zk, k):
        chip = ((self.z + zk) % self.nz) * PLANE + (self.p + k) % PLANE
        block = self.buf.at[core, chip]
        remote(
            block, block, self.csend.at[zk, k], self.recv.at[core, chip], self.chip * 2 + 1 - self.core
        ).wait_recv()

    def second(self):
        def body(zk):
            self.await_block(self.core, zk, 0)
            self.spread(zk)

        each(1, self.nz, body)

    def third(self):
        def body(zk):
            for k in range(1, PLANE):
                self.await_block(self.core, zk, k)
                self.ccopy(zk, k).start()

        each(0, self.nz, body)

    def last(self):
        def body(zk):
            for k in range(PLANE):
                self.await_block(1 - self.core, zk, k)
                self.ccopy(zk, k).wait_send()
            for k in range(1, PLANE):
                self.pcopy(zk, k).wait_send()

        each(0, self.nz, body)
        each(1, self.nz, lambda k: self.zcopy(k).wait_send())


class Exchange:
    def __init__(self, part, other, joined, landed, one, send, recv, place):
        self.part, self.other, self.joined, self.landed = part, other, joined, landed
        self.one, self.send, self.recv = one, send, recv
        self.chip, self.core, unused = place
        self.count = landed.shape[0]

    def inside(self):
        return remote(
            self.part.at[1 - self.core],
            self.other,
            self.one.at[0],
            self.one.at[1],
            self.chip * 2 + 1 - self.core,
        )

    def outside(self, k):
        to = (self.chip + k) % self.count
        return remote(
            self.joined.at[to],
            self.landed.at[self.chip],
            self.send.at[k],
            self.recv.at[self.chip],
            to * 2 + self.core,
        )

    def arrival(self, k):
        origin = (self.chip + self.count - k) % self.count
        return remote(
            self.joined.at[origin],
            self.landed.at[origin],
            self.send.at[k],
            self.recv.at[origin],
            origin * 2 + self.core,
        )

    def go(self, join):
        self.inside().wait_recv()
        self.joined[...] = join(self.part[self.core], self.other[...]).astype(self.joined.dtype)
        each(1, self.count, lambda k: self.outside(k).start())
        self.landed[self.chip] = self.joined[self.chip]

    def finish(self):
        each(1, self.count, lambda k: self.arrival(k).wait_recv())

    def drain(self):
        self.inside().wait_send()
        each(1, self.count, lambda k: self.outside(k).wait_send())


def join_blocks(a, b, width):
    outs = []
    lane = lax.broadcasted_iota(jnp.int32, a.shape[:2] + (128,), 2)
    stats = jnp.zeros(a.shape[:2] + (128,), F32)

    def put(stats, at, value, parts):
        for i in range(parts):
            part = value.astype(BF16).astype(F32)
            stats = jnp.where(lane == at + 8 * i, part, stats)
            value = value - part
        return stats

    for j in range(width // HD):
        ma, mb = a[:, :, width + j : width + j + 1], b[:, :, width + j : width + j + 1]
        sa, sb = (
            a[:, :, width + 64 + j : width + 65 + j],
            b[:, :, width + 64 + j : width + 65 + j],
        )
        top = jnp.maximum(ma, mb)
        ca, cb = jnp.exp(ma - top), jnp.exp(mb - top)
        outs.append(a[:, :, j * HD : (j + 1) * HD] * ca + b[:, :, j * HD : (j + 1) * HD] * cb)
        stats = put(stats, j, top, 3)
        stats = put(stats, 64 + j, sa * ca + sb * cb, 2)
    return jnp.concatenate(outs + [stats], axis=-1)


def rotated(values, cosine, sine):
    return values * cosine + jnp.concatenate([values[:, 64:], values[:, :64]], axis=1) * sine


def kernel(
    count,
    qw,
    hidden_ref,
    gain_ref,
    wq_hbm,
    wk_hbm,
    wv_hbm,
    wo_hbm,
    qa_ref,
    oa_ref,
    bq_ref,
    bo_ref,
    cos_ref,
    sin_ref,
    objective_ref,
    lengths_ref,
    k_hbm,
    v_hbm,
    qout_hbm,
    oout_hbm,
    att_ref,
    wq_ref,
    wk_ref,
    wv_ref,
    wo_ref,
    k_ref,
    v_ref,
    qout_ref,
    oout_ref,
    a_wide,
    a_ref,
    bq_wide,
    bo_wide,
    normed_ref,
    x_ref,
    ra,
    rq,
    ro,
    qg,
    q_part,
    q_other,
    q_joined,
    q_landed,
    kv_part,
    kv_other,
    kv_joined,
    kv_landed,
    m_part,
    m_other,
    m_joined,
    m_landed,
    o_part,
    o_other,
    o_joined,
    o_landed,
    a_send,
    a_recv,
    rq_z,
    rq_p,
    rq_c,
    rq_recv,
    ro_z,
    ro_p,
    ro_c,
    ro_recv,
    g_send,
    g_recv,
    ex_one,
    ex_send,
    ex_recv,
    loads,
    stores,
):
    me = lax.axis_index("tensor")
    chip, core = me // 2, me % 2
    chips = count // 2
    place = (chip, core, chips // PLANE)
    sibling = chip * 2 + 1 - core
    fq, fo = wq_ref.shape[0], wo_ref.shape[0]
    own = qa_ref.shape[0]
    chunks = 16 // own
    rows = count * 16
    width = wo_ref.shape[1]

    barrier = pltpu.get_barrier_semaphore()
    each(
        1,
        count,
        lambda k: pl.semaphore_signal(
            barrier, inc=1, device_id={"tensor": (me + k) % count}
        ),
    )
    pairs = (
        (wq_hbm, wq_ref),
        (wk_hbm, wk_ref),
        (wv_hbm, wv_ref),
        (k_hbm, k_ref),
        (v_hbm, v_ref),
        (wo_hbm, wo_ref),
    )
    fetches = [pltpu.make_async_copy(a, b, loads.at[i]) for i, (a, b) in enumerate(pairs)]
    for fetch in fetches:
        fetch.start()
    for source, wide, buf in ((bq_ref, bq_wide, rq), (bo_ref, bo_wide, ro)):
        step = wide.shape[1]
        factor = source[...].astype(F32)
        for chunk in range(chunks):
            wide[chunk * own : (chunk + 1) * own, :] = factor[:, chunk * step : (chunk + 1) * step]
        buf[core, chip] = wide[...].astype(BF16)
    pl.semaphore_wait(barrier, count - 1)

    gq = Gather(rq, rq_z, rq_p, rq_c, rq_recv, place)
    go = Gather(ro, ro_z, ro_p, ro_c, ro_recv, place)
    gq.first()

    mix = objective_ref[me * own // ADAPTER_RANK].astype(F32) * (ADAPTER_SCALE / WEIGHT_DIVISOR)
    a_wide[...] = jnp.zeros(a_wide.shape, F32)
    skip = 0
    for source, size in ((qa_ref, fq), (oa_ref, fo)):
        factor = source[...].astype(F32) * mix
        for low in range(0, size, 128):
            high = min(size, low + 128)
            for d in range(count):
                a_wide[d, skip * own : (skip + 1) * own, : high - low] = factor[
                    :, d * size + low : d * size + high
                ]
            skip += 1
    a_ref[...] = a_wide[...].astype(BF16)
    ra[core, chip] = a_ref[me]

    def acopy(k):
        to = (me + k) % count
        return remote(a_ref.at[to], ra.at[core, chip], a_send.at[k], a_recv.at[me], to)

    def aarrival(k):
        origin = (me + count - k) % count
        return remote(
            a_ref.at[origin],
            ra.at[origin % 2, origin // 2],
            a_send.at[k],
            a_recv.at[origin],
            origin,
        )

    each(1, count, lambda k: acopy(k).start())
    gq.second()
    go.first()

    hidden = hidden_ref[...].astype(F32)
    hidden = jnp.concatenate([hidden[0], hidden[1]], axis=0)
    spread = lax.rsqrt(jnp.mean(hidden * hidden, axis=1, keepdims=True) + EPS)
    normed_ref[...] = (hidden * spread * gain_ref[...]).astype(BF16).astype(F32)
    for d in range(count):

        @pl.when(me == d)
        def _(d=d):
            x_ref[...] = normed_ref[:, d * fq : (d + 1) * fq].astype(BF16)

    gq.third()
    go.second()
    each(1, count, lambda k: aarrival(k).wait_recv())
    factors = ra[...].reshape(rows, 128).astype(F32).T
    lane = lax.broadcasted_iota(jnp.int32, (128, rows), 1)

    def left(block, chunk, height):
        moved = factors if chunk == block else pltpu.roll(
            factors, ((chunk - block) * own) % rows, 1
        )
        return jnp.where(lane // own % chunks == chunk, moved, 0.0).astype(BF16)[:height]

    def merge(base, out, gathered, features, skip):
        step = gathered.shape[3]
        for block in range(ceil_to(features, 128) // 128):
            low = block * 128
            high = min(features, low + 128)
            for chunk in range(chunks):
                lhs = left(skip + block, chunk, high - low)
                part = step // max(1, step // 512)
                for at in range(0, step, part):
                    right = gathered[:, :, :, at : at + part].reshape(rows, part)
                    span = slice(chunk * step + at, chunk * step + at + part)
                    out[low:high, span] = (base[low:high, span].astype(F32) + dot(lhs, right)).astype(
                        BF16
                    )

    gq.last()
    fetches[0].wait()
    merge(wq_ref, qout_ref, rq, fq, 0)
    keep_q = pltpu.make_async_copy(qout_ref, qout_hbm, stores.at[0])
    keep_q.start()

    ex_q = Exchange(q_part, q_other, q_joined, q_landed, ex_one.at[0], ex_send.at[0], ex_recv.at[0], place)
    ex_kv = Exchange(
        kv_part, kv_other, kv_joined, kv_landed, ex_one.at[1], ex_send.at[1], ex_recv.at[1], place
    )
    ex_m = Exchange(m_part, m_other, m_joined, m_landed, ex_one.at[2], ex_send.at[2], ex_recv.at[2], place)
    ex_o = Exchange(o_part, o_other, o_joined, o_landed, ex_one.at[3], ex_send.at[3], ex_recv.at[3], place)

    x = x_ref[...]
    for d in range(count):
        head = d * HEADS // count
        q_part[d % 2, d // 2] = dot(x, qout_ref[:, head * HD : head * HD + qw])
    ex_q.inside().start()
    for fetch in fetches[1:5]:
        fetch.wait()
    new_k = dot(x, wk_ref[...])
    new_v = dot(x, wv_ref[...])
    for d in range(count):
        g = d * HEADS // count // GROUP
        kv_part[d % 2, d // 2] = jnp.concatenate(
            [new_k[:, g * HD : (g + 1) * HD], new_v[:, g * HD : (g + 1) * HD]], axis=1
        )
    ex_q.go(lambda a, b: a + b)
    ex_kv.inside().start()
    go.third()
    ex_kv.go(lambda a, b: a + b)
    o_part[...] = jnp.zeros(o_part.shape, F32)
    ex_q.finish()
    cosine, sine = cos_ref[...], sin_ref[...]
    query = jnp.sum(q_landed[...], axis=0).astype(BF16).astype(F32)
    query = jnp.concatenate(
        [rotated(query[:, j * HD : (j + 1) * HD], cosine, sine) for j in range(qw // HD)], axis=1
    ).astype(BF16)
    qg[core, chip] = query

    def gcopy(k):
        to = (chip + k) % chips
        block = qg.at[core, chip]
        return remote(block, block, g_send.at[k], g_recv.at[chip], to * 2 + core)

    def garrival(k):
        origin = (chip + chips - k) % chips
        block = qg.at[core, origin]
        return remote(block, block, g_send.at[k], g_recv.at[origin], origin * 2 + core)

    gin = remote(qg.at[core], qg.at[core], g_send.at[0], g_recv.at[chips], sibling)
    gout = remote(qg.at[1 - core], qg.at[1 - core], g_send.at[0], g_recv.at[chips], sibling)
    each(1, chips, lambda k: gcopy(k).start())
    each(1, chips, lambda k: garrival(k).wait_recv())
    gin.start()
    gout.wait_recv()

    scale = HD ** (-0.5)
    decoded, block = k_ref.shape[0], k_ref.shape[1]
    cached = decoded * block
    line = lax.broadcasted_iota(jnp.int32, (GROUP * 16, cached), 0) % decoded
    spot = lax.broadcasted_iota(jnp.int32, (GROUP * 16, cached), 1)
    limit = jnp.zeros((GROUP * 16, cached), jnp.int32)
    for r in range(decoded):
        limit = jnp.where(line == r, lengths_ref[r], limit)
    inside = (me * block + spot % block < limit) & (spot // block == line)
    valid = inside.astype(F32)
    small = lax.broadcasted_iota(jnp.int32, (16, 128), 1)
    per = qw // HD
    for g in range(KVH):
        heads = []
        for h in range(g * GROUP, (g + 1) * GROUP):
            d = h * count // HEADS
            j = h - d * HEADS // count
            heads.append(qg[d % 2, d // 2, :, j * HD : (j + 1) * HD])
        keys = k_ref[:, :, g * HD : (g + 1) * HD].reshape(cached, HD)
        values = v_ref[:, :, g * HD : (g + 1) * HD].reshape(cached, HD)
        scores = (
            lax.dot_general(
                jnp.concatenate(heads, axis=0),
                keys,
                (((1,), (1,)), ((), ())),
                preferred_element_type=F32,
            )
            * scale
        )
        scores = jnp.where(inside, scores, NEG)
        block_max = jnp.max(scores, axis=1, keepdims=True)
        block_exp = jnp.exp(scores - block_max) * valid
        block_sum = jnp.sum(block_exp, axis=1, keepdims=True)
        block_out = dot(block_exp.astype(BF16), values)
        for d in range(count):
            head = d * HEADS // count
            if head // GROUP != g:
                continue
            stats = jnp.zeros((16, 128), F32)
            pieces = []
            for j in range(per):
                span = slice((head + j - g * GROUP) * 16, (head + j - g * GROUP + 1) * 16)
                pieces.append(block_out[span])
                stats = jnp.where(small == j, block_max[span], stats)
                stats = jnp.where(small == 64 + j, block_sum[span], stats)
            m_part[d % 2, d // 2] = jnp.concatenate(pieces + [stats], axis=1)
    ex_m.inside().start()
    ex_m.go(functools.partial(join_blocks, width=qw))

    go.last()
    fetches[5].wait()
    merge(wo_ref, oout_ref, ro, fo, ceil_to(fq, 128) // 128)
    keep_o = pltpu.make_async_copy(oout_ref, oout_hbm, stores.at[1])
    keep_o.start()

    ex_kv.finish()
    fresh = jnp.sum(kv_landed[...], axis=0).astype(BF16).astype(F32)
    new_key = rotated(fresh[:, :HD], cosine, sine).astype(BF16).astype(F32)
    new_value = fresh[:, HD:]
    row = lax.broadcasted_iota(jnp.int32, (16, 1), 0)
    twice = lambda part: jnp.concatenate([part, part], axis=0)
    k0, k1 = twice(new_key[:8]), twice(new_key[8:])
    v0, v1 = twice(new_value[:8]), twice(new_value[8:])
    ex_m.finish()
    landed = m_landed[...].astype(F32)
    pieces = []
    for j in range(per):
        own = query[:, j * HD : (j + 1) * HD].astype(F32)
        s0 = jnp.sum(own * k0, axis=1, keepdims=True) * scale
        s1 = jnp.sum(own * k1, axis=1, keepdims=True) * scale
        s1 = jnp.where(row < 8, NEG, s1)
        parts = [landed[:, :, qw + at + j : qw + at + j + 1] for at in (0, 8, 16, 64, 72)]
        maxima = parts[0] + parts[1] + parts[2]
        top = jnp.maximum(jnp.max(maxima, axis=0), jnp.maximum(s0, s1))
        carried = jnp.exp(maxima - top[None])
        e0, e1 = jnp.exp(s0 - top), jnp.exp(s1 - top)
        total = jnp.sum((parts[3] + parts[4]) * carried, axis=0) + e0 + e1
        upper = jnp.sum(landed[:, :, j * HD : (j + 1) * HD] * carried, axis=0) + e0 * v0 + e1 * v1
        pieces.append((upper / total).astype(BF16))
    attention = jnp.concatenate(pieces, axis=1)
    if fo < qw:
        attention = jnp.where(me % (qw // fo) == 0, attention[:, :fo], attention[:, fo : 2 * fo])

    share = width // count
    for d in range(0, count, 4):
        wide = dot(attention, oout_ref[:, d * share : (d + 4) * share])
        for i in range(4):
            o_part[(d + i) % 2, (d + i) // 2, :, :share] = wide[:, i * share : (i + 1) * share]
    ex_o.inside().start()
    ex_o.go(lambda a, b: a + b)
    ex_o.finish()
    att_ref[...] = jnp.sum(o_landed[...].astype(F32), axis=0)[:, :share].astype(BF16)

    each(1, count, lambda k: acopy(k).wait_send())
    each(1, chips, lambda k: gcopy(k).wait_send())
    gin.wait_send()
    for exchange in (ex_q, ex_kv, ex_m, ex_o):
        exchange.drain()
    keep_q.wait()
    keep_o.wait()


def local(
    incoming_hidden,
    norm_weight_vector,
    query_matrix,
    key_matrix,
    value_matrix,
    output_matrix,
    query_adapter_input,
    query_adapter_output,
    output_adapter_input,
    output_adapter_output,
    objective_numerators,
    lengths,
    stored_keys,
    stored_values,
):
    count = lax.axis_size("tensor")
    steps, rows, features = incoming_hidden.shape
    lines = steps * rows
    own = query_adapter_input.shape[0]
    chunks = 16 // own
    fq, fo = query_matrix.shape[0], output_matrix.shape[0]
    columns = query_matrix.shape[1]
    qw = max(HD, columns // count)
    chips = count // 2
    nz = chips // PLANE

    half = np.arange(HD) % (HD // 2)
    frequency = (THETA ** (-2.0 * half / HD)).astype(np.float32)
    sign = np.where(np.arange(HD) < HD // 2, -1.0, 1.0).astype(np.float32)
    positions = lengths[None, :] + jnp.arange(steps, dtype=jnp.int32)[:, None]
    angle = positions.astype(F32)[..., None] * frequency
    cosine = jnp.cos(angle).reshape(lines, HD)
    sine = (jnp.sin(angle) * sign).reshape(lines, HD)

    share = output_matrix.shape[1] // count
    ow = ceil_to(share, 128)
    vmem = pl.BlockSpec(memory_space=pltpu.VMEM)
    smem = pl.BlockSpec(memory_space=pltpu.SMEM)
    hbm = pl.BlockSpec(memory_space=pl.ANY)
    wide_q, wide_o = columns // chunks, output_matrix.shape[1] // chunks
    dma = pltpu.SemaphoreType.DMA

    def exchange(width, sent=F32):
        return [
            pltpu.VMEM((2, chips, lines, width), F32),
            pltpu.VMEM((chips, lines, width), F32),
            pltpu.VMEM((chips, lines, width), sent),
            pltpu.VMEM((chips, lines, width), sent),
        ]

    def gather():
        return [dma((nz,)), dma((nz, PLANE)), dma((nz, PLANE)), dma((2, chips))]

    query_out, output_out, attended = pl.pallas_call(
        functools.partial(kernel, count, qw),
        out_shape=(
            jax.ShapeDtypeStruct(query_matrix.shape, BF16),
            jax.ShapeDtypeStruct(output_matrix.shape, BF16),
            jax.ShapeDtypeStruct((lines, share), BF16),
        ),
        in_specs=[vmem] * 2 + [hbm] * 4 + [vmem] * 6 + [smem] * 2 + [hbm] * 2,
        out_specs=(hbm, hbm, vmem),
        scratch_shapes=[
            pltpu.VMEM(query_matrix.shape, BF16),
            pltpu.VMEM(key_matrix.shape, BF16),
            pltpu.VMEM(value_matrix.shape, BF16),
            pltpu.VMEM(output_matrix.shape, BF16),
            pltpu.VMEM(stored_keys.shape, BF16),
            pltpu.VMEM(stored_values.shape, BF16),
            pltpu.VMEM(query_matrix.shape, BF16),
            pltpu.VMEM(output_matrix.shape, BF16),
            pltpu.VMEM((count, 16, 128), F32),
            pltpu.VMEM((count, 16, 128), BF16),
            pltpu.VMEM((16, wide_q), F32),
            pltpu.VMEM((16, wide_o), F32),
            pltpu.VMEM((lines, features), F32),
            pltpu.VMEM((lines, fq), BF16),
            pltpu.VMEM((2, chips, 16, 128), BF16),
            pltpu.VMEM((2, chips, 16, wide_q), BF16),
            pltpu.VMEM((2, chips, 16, wide_o), BF16),
            pltpu.VMEM((2, chips, lines, qw), BF16),
        ]
        + exchange(qw)
        + exchange(2 * HD)
        + exchange(qw + 128, BF16)
        + exchange(ow, BF16)
        + [dma((count,)), dma((count,))]
        + gather()
        + gather()
        + [dma((chips,)), dma((chips + 1,))]
        + [dma((4, 2)), dma((4, chips)), dma((4, chips))]
        + [dma((6,)), dma((2,))],
        compiler_params=pltpu.CompilerParams(
            collective_id=0, has_side_effects=True, vmem_limit_bytes=56 * 1024 * 1024
        ),
    )(
        incoming_hidden,
        norm_weight_vector.reshape(1, features),
        query_matrix,
        key_matrix,
        value_matrix,
        output_matrix,
        query_adapter_input,
        output_adapter_input,
        query_adapter_output,
        output_adapter_output,
        cosine,
        sine,
        objective_numerators,
        lengths,
        stored_keys,
        stored_values,
    )
    return (query_out, output_out, attended.reshape(steps, rows, share))


def solution(mesh):
    placed = (
        P(None, "groups", None),
        P(),
        P("tensor", None),
        P("tensor", None),
        P("tensor", None),
        P("tensor", None),
        P("tensor", None),
        P("tensor", None),
        P("tensor", None),
        P("tensor", None),
        P("groups"),
        P("groups"),
        P("groups", "tensor", None),
        P("groups", "tensor", None),
    )
    return jax.shard_map(
        local,
        mesh=mesh,
        in_specs=placed,
        out_specs=(
            P(("groups", "tensor"), None),
            P("tensor", "groups"),
            P(None, "groups", "tensor"),
        ),
        check_vma=False,
    )
```

```python
import functools

import jax
import jax.numpy as jnp
import numpy as np
from jax import lax
from jax.experimental import pallas as pl
from jax.experimental.pallas import tpu as pltpu
from jax.sharding import PartitionSpec as P

HEADS = 64
KVH = 8
HD = 128
ADAPTER_RANK = 32
WEIGHT_DIVISOR = 16
GROUP = HEADS // KVH
PLANE = 4

ADAPTER_SCALE = 2.0
THETA = 1000000.0
EPS = 1e-06
NEG = -1e30
F32 = jnp.float32
BF16 = jnp.bfloat16


def ceil_to(value, step):
    return -(-value // step) * step


def dot(a, b):
    return jnp.dot(a, b, preferred_element_type=F32)


def remote(src, dst, send, recv, device):
    return pltpu.make_async_remote_copy(
        src_ref=src, dst_ref=dst, send_sem=send, recv_sem=recv, device_id={"tensor": device}
    )


def each(first, last, body):
    def step(k, carry):
        body(k)
        return carry

    lax.fori_loop(first, last, step, 0)


class Gather:
    def __init__(self, buf, zsend, psend, csend, recv, halves, place):
        self.buf, self.zsend, self.psend, self.csend, self.recv = buf, zsend, psend, csend, recv
        self.halves = halves
        self.halved = (1, 2) if buf.shape[3] % 256 == 0 else (1,)
        self.chip, self.core, self.nz = place
        self.z, self.p = self.chip // PLANE, self.chip % PLANE

    def copy(self, chip, send, device):
        block = self.buf.at[self.core, chip]
        return remote(block, block, send, self.recv.at[self.core, chip], device)

    def zcopy(self, k):
        z = (self.z + k) % self.nz
        return self.copy(self.chip, self.zsend.at[k - 1], (z * PLANE + self.p) * 2 + self.core)

    def chip_of(self, zk, k):
        p = (self.p, self.p + 1 - self.p % 2 * 2, (self.p + 2) % PLANE, PLANE - 1 - self.p)[k]
        return ((self.z + zk) % self.nz) * PLANE + p

    def pcopy(self, zk, k):
        return self.copy(
            self.chip_of(zk, 0), self.psend.at[zk, k - 1], self.chip_of(0, k) * 2 + self.core
        )

    def half(self, chip, k):
        if len(self.halved) == 1:
            return self.buf.at[self.core, chip]
        size = self.buf.shape[3] // 2
        return self.buf.at[self.core, chip, :, pl.ds((k - 1) * size, size)]

    def forward(self, zk, k):
        chip = self.chip_of(zk, k)
        block = self.half(chip, k)
        return remote(
            block,
            block,
            self.psend.at[zk, k + 1],
            self.halves.at[chip, k - 1],
            self.chip_of(0, 3 - k) * 2 + self.core,
        )

    def await_half(self, zk, k):
        chip = self.chip_of(zk, 3)
        block = self.half(chip, k)
        remote(
            block,
            block,
            self.psend.at[zk, k + 1],
            self.halves.at[chip, k - 1],
            self.chip_of(0, 3 - k) * 2 + self.core,
        ).wait_recv()

    def ccopy(self, zk, k):
        return self.copy(
            self.chip_of(zk, k), self.csend.at[zk, k], self.chip * 2 + 1 - self.core
        )

    def first(self):
        each(1, self.nz, lambda k: self.zcopy(k).start())
        self.spread(0)

    def spread(self, zk):
        for k in (1, 2):
            self.pcopy(zk, k).start()
        self.ccopy(zk, 0).start()

    def await_block(self, core, zk, k):
        chip = self.chip_of(zk, k)
        block = self.buf.at[core, chip]
        remote(
            block, block, self.csend.at[zk, k], self.recv.at[core, chip], self.chip * 2 + 1 - self.core
        ).wait_recv()

    def second(self):
        def body(zk):
            self.await_block(self.core, zk, 0)
            self.spread(zk)

        each(1, self.nz, body)

    def third(self):
        def body(zk):
            for k in (1, 2):
                self.await_block(self.core, zk, k)
                if k in self.halved:
                    self.forward(zk, k).start()
                self.ccopy(zk, k).start()

        def corner(zk):
            for k in self.halved:
                self.await_half(zk, k)
            self.ccopy(zk, 3).start()

        each(0, self.nz, body)
        each(0, self.nz, corner)

    def last(self):
        def body(zk):
            for k in range(PLANE):
                self.await_block(1 - self.core, zk, k)
                self.ccopy(zk, k).wait_send()
            for k in (1, 2):
                self.pcopy(zk, k).wait_send()
                if k in self.halved:
                    self.forward(zk, k).wait_send()

        each(0, self.nz, body)
        each(1, self.nz, lambda k: self.zcopy(k).wait_send())


class Exchange:
    def __init__(self, part, other, joined, landed, one, send, recv, place):
        self.part, self.other, self.joined, self.landed = part, other, joined, landed
        self.one, self.send, self.recv = one, send, recv
        self.chip, self.core, unused = place
        self.count = landed.shape[0]

    def inside(self):
        return remote(
            self.part.at[1 - self.core],
            self.other,
            self.one.at[0],
            self.one.at[1],
            self.chip * 2 + 1 - self.core,
        )

    def outside(self, k):
        to = (self.chip + k) % self.count
        return remote(
            self.joined.at[to],
            self.landed.at[self.chip],
            self.send.at[k],
            self.recv.at[self.chip],
            to * 2 + self.core,
        )

    def arrival(self, k):
        origin = (self.chip + self.count - k) % self.count
        return remote(
            self.joined.at[origin],
            self.landed.at[origin],
            self.send.at[k],
            self.recv.at[origin],
            origin * 2 + self.core,
        )

    def go(self, join):
        self.inside().wait_recv()
        self.joined[...] = join(self.part[self.core], self.other[...]).astype(self.joined.dtype)
        each(1, self.count, lambda k: self.outside(k).start())
        self.landed[self.chip] = self.joined[self.chip]

    def finish(self):
        each(1, self.count, lambda k: self.arrival(k).wait_recv())

    def drain(self):
        self.inside().wait_send()
        each(1, self.count, lambda k: self.outside(k).wait_send())


def join_blocks(a, b, width):
    outs = []
    lane = lax.broadcasted_iota(jnp.int32, a.shape[:2] + (128,), 2)
    stats = jnp.zeros(a.shape[:2] + (128,), F32)

    def put(stats, at, value, parts):
        for i in range(parts):
            part = value.astype(BF16).astype(F32)
            stats = jnp.where(lane == at + 8 * i, part, stats)
            value = value - part
        return stats

    for j in range(width // HD):
        ma, mb = a[:, :, width + j : width + j + 1], b[:, :, width + j : width + j + 1]
        sa, sb = (
            a[:, :, width + 64 + j : width + 65 + j],
            b[:, :, width + 64 + j : width + 65 + j],
        )
        top = jnp.maximum(ma, mb)
        ca, cb = jnp.exp(ma - top), jnp.exp(mb - top)
        outs.append(a[:, :, j * HD : (j + 1) * HD] * ca + b[:, :, j * HD : (j + 1) * HD] * cb)
        stats = put(stats, j, top, 3)
        stats = put(stats, 64 + j, sa * ca + sb * cb, 2)
    return jnp.concatenate(outs + [stats], axis=-1)


def rotated(values, cosine, sine):
    return values * cosine + jnp.concatenate([values[:, 64:], values[:, :64]], axis=1) * sine


def kernel(
    count,
    qw,
    hidden_ref,
    gain_ref,
    wq_hbm,
    wk_hbm,
    wv_hbm,
    wo_hbm,
    qa_ref,
    oa_ref,
    bq_ref,
    bo_ref,
    cos_ref,
    sin_ref,
    objective_ref,
    lengths_ref,
    k_hbm,
    v_hbm,
    qout_hbm,
    oout_hbm,
    att_ref,
    wq_ref,
    wk_ref,
    wv_ref,
    wo_ref,
    k_ref,
    v_ref,
    qout_ref,
    oout_ref,
    a_wide,
    a_ref,
    bq_wide,
    bo_wide,
    normed_ref,
    x_ref,
    ra,
    rq,
    ro,
    qg,
    q_part,
    q_other,
    q_joined,
    q_landed,
    kv_part,
    kv_other,
    kv_joined,
    kv_landed,
    m_part,
    m_other,
    m_joined,
    m_landed,
    o_part,
    o_other,
    o_joined,
    o_landed,
    a_send,
    a_recv,
    rq_z,
    rq_p,
    rq_c,
    rq_recv,
    rq_half,
    ro_z,
    ro_p,
    ro_c,
    ro_recv,
    ro_half,
    g_send,
    g_recv,
    ex_one,
    ex_send,
    ex_recv,
    loads,
    stores,
):
    me = lax.axis_index("tensor")
    chip, core = me // 2, me % 2
    chips = count // 2
    place = (chip, core, chips // PLANE)
    sibling = chip * 2 + 1 - core
    fq, fo = wq_ref.shape[0], wo_ref.shape[0]
    own = qa_ref.shape[0]
    chunks = 16 // own
    rows = count * 16
    width = wo_ref.shape[1]

    barrier = pltpu.get_barrier_semaphore()
    each(
        1,
        count,
        lambda k: pl.semaphore_signal(
            barrier, inc=1, device_id={"tensor": (me + k) % count}
        ),
    )
    pairs = (
        (wq_hbm, wq_ref),
        (wk_hbm, wk_ref),
        (wv_hbm, wv_ref),
        (k_hbm, k_ref),
        (v_hbm, v_ref),
        (wo_hbm, wo_ref),
    )
    fetches = [pltpu.make_async_copy(a, b, loads.at[i]) for i, (a, b) in enumerate(pairs)]
    for fetch in fetches:
        fetch.start()
    for source, wide, buf in ((bq_ref, bq_wide, rq), (bo_ref, bo_wide, ro)):
        step = wide.shape[1]
        factor = source[...].astype(F32)
        for chunk in range(chunks):
            wide[chunk * own : (chunk + 1) * own, :] = factor[:, chunk * step : (chunk + 1) * step]
        buf[core, chip] = wide[...].astype(BF16)
    pl.semaphore_wait(barrier, count - 1)

    gq = Gather(rq, rq_z, rq_p, rq_c, rq_recv, rq_half, place)
    go = Gather(ro, ro_z, ro_p, ro_c, ro_recv, ro_half, place)
    gq.first()

    mix = objective_ref[me * own // ADAPTER_RANK].astype(F32) * (ADAPTER_SCALE / WEIGHT_DIVISOR)
    a_wide[...] = jnp.zeros(a_wide.shape, F32)
    skip = 0
    for source, size in ((qa_ref, fq), (oa_ref, fo)):
        factor = source[...].astype(F32) * mix
        for low in range(0, size, 128):
            high = min(size, low + 128)
            for d in range(count):
                a_wide[d, skip * own : (skip + 1) * own, : high - low] = factor[
                    :, d * size + low : d * size + high
                ]
            skip += 1
    a_ref[...] = a_wide[...].astype(BF16)
    ra[core, chip] = a_ref[me]

    def acopy(k):
        to = (me + k) % count
        return remote(a_ref.at[to], ra.at[core, chip], a_send.at[k], a_recv.at[me], to)

    def aarrival(k):
        origin = (me + count - k) % count
        return remote(
            a_ref.at[origin],
            ra.at[origin % 2, origin // 2],
            a_send.at[k],
            a_recv.at[origin],
            origin,
        )

    each(1, count, lambda k: acopy(k).start())
    gq.second()
    go.first()

    hidden = hidden_ref[...].astype(F32)
    hidden = jnp.concatenate([hidden[0], hidden[1]], axis=0)
    spread = lax.rsqrt(jnp.mean(hidden * hidden, axis=1, keepdims=True) + EPS)
    normed_ref[...] = (hidden * spread * gain_ref[...]).astype(BF16).astype(F32)
    for d in range(count):

        @pl.when(me == d)
        def _(d=d):
            x_ref[...] = normed_ref[:, d * fq : (d + 1) * fq].astype(BF16)

    gq.third()
    go.second()
    each(1, count, lambda k: aarrival(k).wait_recv())
    factors = ra[...].reshape(rows, 128).astype(F32).T
    lane = lax.broadcasted_iota(jnp.int32, (128, rows), 1)

    def left(block, chunk, height):
        moved = factors if chunk == block else pltpu.roll(
            factors, ((chunk - block) * own) % rows, 1
        )
        return jnp.where(lane // own % chunks == chunk, moved, 0.0).astype(BF16)[:height]

    def merge(base, out, gathered, features, skip):
        step = gathered.shape[3]
        for block in range(ceil_to(features, 128) // 128):
            low = block * 128
            high = min(features, low + 128)
            for chunk in range(chunks):
                lhs = left(skip + block, chunk, high - low)
                part = step // max(1, step // 512)
                for at in range(0, step, part):
                    right = gathered[:, :, :, at : at + part].reshape(rows, part)
                    span = slice(chunk * step + at, chunk * step + at + part)
                    out[low:high, span] = (base[low:high, span].astype(F32) + dot(lhs, right)).astype(
                        BF16
                    )

    gq.last()
    fetches[0].wait()
    merge(wq_ref, qout_ref, rq, fq, 0)
    keep_q = pltpu.make_async_copy(qout_ref, qout_hbm, stores.at[0])
    keep_q.start()

    ex_q = Exchange(q_part, q_other, q_joined, q_landed, ex_one.at[0], ex_send.at[0], ex_recv.at[0], place)
    ex_kv = Exchange(
        kv_part, kv_other, kv_joined, kv_landed, ex_one.at[1], ex_send.at[1], ex_recv.at[1], place
    )
    ex_m = Exchange(m_part, m_other, m_joined, m_landed, ex_one.at[2], ex_send.at[2], ex_recv.at[2], place)
    ex_o = Exchange(o_part, o_other, o_joined, o_landed, ex_one.at[3], ex_send.at[3], ex_recv.at[3], place)

    x = x_ref[...]
    for d in range(count):
        head = d * HEADS // count
        q_part[d % 2, d // 2] = dot(x, qout_ref[:, head * HD : head * HD + qw])
    ex_q.inside().start()
    for fetch in fetches[1:5]:
        fetch.wait()
    new_k = dot(x, wk_ref[...])
    new_v = dot(x, wv_ref[...])
    for d in range(count):
        g = d * HEADS // count // GROUP
        kv_part[d % 2, d // 2] = jnp.concatenate(
            [new_k[:, g * HD : (g + 1) * HD], new_v[:, g * HD : (g + 1) * HD]], axis=1
        )
    ex_q.go(lambda a, b: a + b)
    ex_kv.inside().start()
    go.third()
    ex_kv.go(lambda a, b: a + b)
    o_part[...] = jnp.zeros(o_part.shape, F32)
    ex_q.finish()
    cosine, sine = cos_ref[...], sin_ref[...]
    query = jnp.sum(q_landed[...], axis=0).astype(BF16).astype(F32)
    query = jnp.concatenate(
        [rotated(query[:, j * HD : (j + 1) * HD], cosine, sine) for j in range(qw // HD)], axis=1
    ).astype(BF16)
    qg[core, chip] = query

    def gcopy(k):
        to = (chip + k) % chips
        block = qg.at[core, chip]
        return remote(block, block, g_send.at[k], g_recv.at[chip], to * 2 + core)

    def garrival(k):
        origin = (chip + chips - k) % chips
        block = qg.at[core, origin]
        return remote(block, block, g_send.at[k], g_recv.at[origin], origin * 2 + core)

    gin = remote(qg.at[core], qg.at[core], g_send.at[0], g_recv.at[chips], sibling)
    gout = remote(qg.at[1 - core], qg.at[1 - core], g_send.at[0], g_recv.at[chips], sibling)
    each(1, chips, lambda k: gcopy(k).start())
    each(1, chips, lambda k: garrival(k).wait_recv())
    gin.start()
    gout.wait_recv()

    scale = HD ** (-0.5)
    decoded, block = k_ref.shape[0], k_ref.shape[1]
    cached = decoded * block
    line = lax.broadcasted_iota(jnp.int32, (GROUP * 16, cached), 0) % decoded
    spot = lax.broadcasted_iota(jnp.int32, (GROUP * 16, cached), 1)
    limit = jnp.zeros((GROUP * 16, cached), jnp.int32)
    for r in range(decoded):
        limit = jnp.where(line == r, lengths_ref[r], limit)
    inside = (me * block + spot % block < limit) & (spot // block == line)
    valid = inside.astype(F32)
    small = lax.broadcasted_iota(jnp.int32, (16, 128), 1)
    per = qw // HD
    for g in range(KVH):
        heads = []
        for h in range(g * GROUP, (g + 1) * GROUP):
            d = h * count // HEADS
            j = h - d * HEADS // count
            heads.append(qg[d % 2, d // 2, :, j * HD : (j + 1) * HD])
        keys = k_ref[:, :, g * HD : (g + 1) * HD].reshape(cached, HD)
        values = v_ref[:, :, g * HD : (g + 1) * HD].reshape(cached, HD)
        scores = (
            lax.dot_general(
                jnp.concatenate(heads, axis=0),
                keys,
                (((1,), (1,)), ((), ())),
                preferred_element_type=F32,
            )
            * scale
        )
        scores = jnp.where(inside, scores, NEG)
        block_max = jnp.max(scores, axis=1, keepdims=True)
        block_exp = jnp.exp(scores - block_max) * valid
        block_sum = jnp.sum(block_exp, axis=1, keepdims=True)
        block_out = dot(block_exp.astype(BF16), values)
        for d in range(count):
            head = d * HEADS // count
            if head // GROUP != g:
                continue
            stats = jnp.zeros((16, 128), F32)
            pieces = []
            for j in range(per):
                span = slice((head + j - g * GROUP) * 16, (head + j - g * GROUP + 1) * 16)
                pieces.append(block_out[span])
                stats = jnp.where(small == j, block_max[span], stats)
                stats = jnp.where(small == 64 + j, block_sum[span], stats)
            m_part[d % 2, d // 2] = jnp.concatenate(pieces + [stats], axis=1)
    ex_m.inside().start()
    ex_m.go(functools.partial(join_blocks, width=qw))

    go.last()
    fetches[5].wait()
    merge(wo_ref, oout_ref, ro, fo, ceil_to(fq, 128) // 128)
    keep_o = pltpu.make_async_copy(oout_ref, oout_hbm, stores.at[1])
    keep_o.start()

    ex_kv.finish()
    fresh = jnp.sum(kv_landed[...], axis=0).astype(BF16).astype(F32)
    new_key = rotated(fresh[:, :HD], cosine, sine).astype(BF16).astype(F32)
    new_value = fresh[:, HD:]
    row = lax.broadcasted_iota(jnp.int32, (16, 1), 0)
    twice = lambda part: jnp.concatenate([part, part], axis=0)
    k0, k1 = twice(new_key[:8]), twice(new_key[8:])
    v0, v1 = twice(new_value[:8]), twice(new_value[8:])
    ex_m.finish()
    landed = m_landed[...].astype(F32)
    pieces = []
    for j in range(per):
        own = query[:, j * HD : (j + 1) * HD].astype(F32)
        s0 = jnp.sum(own * k0, axis=1, keepdims=True) * scale
        s1 = jnp.sum(own * k1, axis=1, keepdims=True) * scale
        s1 = jnp.where(row < 8, NEG, s1)
        parts = [landed[:, :, qw + at + j : qw + at + j + 1] for at in (0, 8, 16, 64, 72)]
        maxima = parts[0] + parts[1] + parts[2]
        top = jnp.maximum(jnp.max(maxima, axis=0), jnp.maximum(s0, s1))
        carried = jnp.exp(maxima - top[None])
        e0, e1 = jnp.exp(s0 - top), jnp.exp(s1 - top)
        total = jnp.sum((parts[3] + parts[4]) * carried, axis=0) + e0 + e1
        upper = jnp.sum(landed[:, :, j * HD : (j + 1) * HD] * carried, axis=0) + e0 * v0 + e1 * v1
        pieces.append((upper / total).astype(BF16))
    attention = jnp.concatenate(pieces, axis=1)
    if fo < qw:
        attention = jnp.where(me % (qw // fo) == 0, attention[:, :fo], attention[:, fo : 2 * fo])

    share = width // count
    for d in range(0, count, 4):
        wide = dot(attention, oout_ref[:, d * share : (d + 4) * share])
        for i in range(4):
            o_part[(d + i) % 2, (d + i) // 2, :, :share] = wide[:, i * share : (i + 1) * share]
    ex_o.inside().start()
    ex_o.go(lambda a, b: a + b)
    ex_o.finish()
    att_ref[...] = jnp.sum(o_landed[...].astype(F32), axis=0)[:, :share].astype(BF16)

    each(1, count, lambda k: acopy(k).wait_send())
    each(1, chips, lambda k: gcopy(k).wait_send())
    gin.wait_send()
    for exchange in (ex_q, ex_kv, ex_m, ex_o):
        exchange.drain()
    keep_q.wait()
    keep_o.wait()


def local(
    incoming_hidden,
    norm_weight_vector,
    query_matrix,
    key_matrix,
    value_matrix,
    output_matrix,
    query_adapter_input,
    query_adapter_output,
    output_adapter_input,
    output_adapter_output,
    objective_numerators,
    lengths,
    stored_keys,
    stored_values,
):
    count = lax.axis_size("tensor")
    steps, rows, features = incoming_hidden.shape
    lines = steps * rows
    own = query_adapter_input.shape[0]
    chunks = 16 // own
    fq, fo = query_matrix.shape[0], output_matrix.shape[0]
    columns = query_matrix.shape[1]
    qw = max(HD, columns // count)
    chips = count // 2
    nz = chips // PLANE

    half = np.arange(HD) % (HD // 2)
    frequency = (THETA ** (-2.0 * half / HD)).astype(np.float32)
    sign = np.where(np.arange(HD) < HD // 2, -1.0, 1.0).astype(np.float32)
    positions = lengths[None, :] + jnp.arange(steps, dtype=jnp.int32)[:, None]
    angle = positions.astype(F32)[..., None] * frequency
    cosine = jnp.cos(angle).reshape(lines, HD)
    sine = (jnp.sin(angle) * sign).reshape(lines, HD)

    share = output_matrix.shape[1] // count
    ow = ceil_to(share, 128)
    vmem = pl.BlockSpec(memory_space=pltpu.VMEM)
    smem = pl.BlockSpec(memory_space=pltpu.SMEM)
    hbm = pl.BlockSpec(memory_space=pl.ANY)
    wide_q, wide_o = columns // chunks, output_matrix.shape[1] // chunks
    dma = pltpu.SemaphoreType.DMA

    def exchange(width, sent=F32):
        return [
            pltpu.VMEM((2, chips, lines, width), F32),
            pltpu.VMEM((chips, lines, width), F32),
            pltpu.VMEM((chips, lines, width), sent),
            pltpu.VMEM((chips, lines, width), sent),
        ]

    def gather():
        return [dma((nz,)), dma((nz, PLANE)), dma((nz, PLANE)), dma((2, chips)), dma((chips, 2))]

    query_out, output_out, attended = pl.pallas_call(
        functools.partial(kernel, count, qw),
        out_shape=(
            jax.ShapeDtypeStruct(query_matrix.shape, BF16),
            jax.ShapeDtypeStruct(output_matrix.shape, BF16),
            jax.ShapeDtypeStruct((lines, share), BF16),
        ),
        in_specs=[vmem] * 2 + [hbm] * 4 + [vmem] * 6 + [smem] * 2 + [hbm] * 2,
        out_specs=(hbm, hbm, vmem),
        scratch_shapes=[
            pltpu.VMEM(query_matrix.shape, BF16),
            pltpu.VMEM(key_matrix.shape, BF16),
            pltpu.VMEM(value_matrix.shape, BF16),
            pltpu.VMEM(output_matrix.shape, BF16),
            pltpu.VMEM(stored_keys.shape, BF16),
            pltpu.VMEM(stored_values.shape, BF16),
            pltpu.VMEM(query_matrix.shape, BF16),
            pltpu.VMEM(output_matrix.shape, BF16),
            pltpu.VMEM((count, 16, 128), F32),
            pltpu.VMEM((count, 16, 128), BF16),
            pltpu.VMEM((16, wide_q), F32),
            pltpu.VMEM((16, wide_o), F32),
            pltpu.VMEM((lines, features), F32),
            pltpu.VMEM((lines, fq), BF16),
            pltpu.VMEM((2, chips, 16, 128), BF16),
            pltpu.VMEM((2, chips, 16, wide_q), BF16),
            pltpu.VMEM((2, chips, 16, wide_o), BF16),
            pltpu.VMEM((2, chips, lines, qw), BF16),
        ]
        + exchange(qw)
        + exchange(2 * HD)
        + exchange(qw + 128)
        + exchange(ow)
        + [dma((count,)), dma((count,))]
        + gather()
        + gather()
        + [dma((chips,)), dma((chips + 1,))]
        + [dma((4, 2)), dma((4, chips)), dma((4, chips))]
        + [dma((6,)), dma((2,))],
        compiler_params=pltpu.CompilerParams(
            collective_id=0, has_side_effects=True, vmem_limit_bytes=56 * 1024 * 1024
        ),
    )(
        incoming_hidden,
        norm_weight_vector.reshape(1, features),
        query_matrix,
        key_matrix,
        value_matrix,
        output_matrix,
        query_adapter_input,
        output_adapter_input,
        query_adapter_output,
        output_adapter_output,
        cosine,
        sine,
        objective_numerators,
        lengths,
        stored_keys,
        stored_values,
    )
    return (query_out, output_out, attended.reshape(steps, rows, share))


def solution(mesh):
    placed = (
        P(None, "groups", None),
        P(),
        P("tensor", None),
        P("tensor", None),
        P("tensor", None),
        P("tensor", None),
        P("tensor", None),
        P("tensor", None),
        P("tensor", None),
        P("tensor", None),
        P("groups"),
        P("groups"),
        P("groups", "tensor", None),
        P("groups", "tensor", None),
    )
    return jax.shard_map(
        local,
        mesh=mesh,
        in_specs=placed,
        out_specs=(
            P(("groups", "tensor"), None),
            P("tensor", "groups"),
            P(None, "groups", "tensor"),
        ),
        check_vma=False,
    )
```
